128 devices in a mesh: chan: 8 (over y, core), tm: 16 (over x, z).
Axes of the slice: x: 4, y: 4, z: 4, core: 2. Of those that a mesh axis runs over, the one named last changes fastest.
Arguments:
- readings: float32 [16384, 16384], P('chan', 'tm'), may hold values from -8 to 8
- channel_start: float32 [16384, 64], P(('chan', 'tm')), may hold values from -6 to 6
- time_start: float32 [16384, 64], P(('tm', 'chan')), may hold values from -0.75 to 0.75
Outputs:
- outliers: float32 [16384, 16384], P('chan', 'tm')
- channel_factors: float32 [16384, 64], P(('chan', 'tm'))
- time_factors: float32 [16384, 64], P(('tm', 'chan'))
The draws below stay inside these ranges and needn't reach their ends.
All inputs are finite; a program needn't handle non-finite values.
Results may differ from the reference program's by a relative error of at most 0.00019.
Values sent between devices are 32-bit elements; how exact they have to be, the bound alone decides.
No kernel may reach another device: no remote copies, remote signals or barrier semaphores. Data moves between devices by JAX's collectives and lax.ppermute only.
A program may use at most 128 MiB of HBM per device.

```python
import jax
import jax.numpy as jnp
from jax import lax

RANK = 64
ITERS = 2
CHANNELS = 16384
TIMES = 16384


def levels(own_key, shape, pieces, low, top_value):
    factor_of, own = 1.0, jax.random.fold_in(own_key, 6)
    for axis_at, shards_of in pieces:
        heights = jnp.exp(jax.random.uniform(jax.random.fold_in(own, axis_at), (shards_of,), jnp.float32, low / len(pieces), top_value / len(pieces)))
        factor_of = factor_of * jnp.repeat(heights, shape[axis_at] // shards_of).reshape([-1 if axis == axis_at else 1 for axis in range(len(shape))])
    return factor_of


def centred(stream_key, dims, scale, bound, cuts=(), held_as=jnp.bfloat16):
    values = jax.random.normal(stream_key, dims, jnp.float32) * scale
    if len(cuts) > 0:
        values = levels(stream_key, dims, cuts, -0.22, 0.18) * values
    return jnp.clip(values, min=-bound, max=bound).astype(held_as)


def setup_inputs(seed: int = 0) -> dict:
    key_list = jax.random.split(jax.random.key(seed), 4)
    readings = centred(key_list[0], (CHANNELS, TIMES), 1.0, 8.0, ((0, 8), (1, 16)), jnp.float32)
    channel_start = centred(key_list[1], (CHANNELS, RANK), 1.0, 6.0, ((0, 128),), jnp.float32)
    time_start = centred(key_list[2], (TIMES, RANK), RANK ** -0.5, 0.75, ((0, 128),), jnp.float32)
    return dict(readings=readings, channel_start=channel_start, time_start=time_start)


threshold_level = 1.5
ridge_weight = 8.0

def product(first, second):
    return jnp.dot(first.astype(jnp.float32), second.astype(jnp.float32), precision=lax.Precision.HIGHEST, preferred_element_type=jnp.float32)

def solve_ridge(partial_value, gram):
    factor_chol = jnp.linalg.cholesky(gram)
    middle = lax.linalg.triangular_solve(factor_chol, partial_value, left_side=False, lower=True, transpose_a=True)
    return lax.linalg.triangular_solve(factor_chol, middle, left_side=False, lower=True, transpose_a=False)

def reference(readings, channel_start, time_start):
    identity = jnp.eye(RANK, dtype=jnp.float32)
    left_factor = channel_start
    right_factor = time_start
    outliers = readings
    for sweep in range(ITERS):
        residue = readings - product(left_factor, right_factor.T)
        outliers = residue - jnp.clip(residue, -threshold_level, threshold_level)
        cleaned = readings - outliers
        gram_right = product(right_factor.T, right_factor) + ridge_weight * identity
        left_factor = solve_ridge(product(cleaned, right_factor), gram_right)
        gram_left = product(left_factor.T, left_factor) + ridge_weight * identity
        right_factor = solve_ridge(product(cleaned.T, left_factor), gram_left)
    return (outliers, left_factor, right_factor)
```

```python
import functools

import jax
import jax.numpy as jnp
from jax import lax
from jax.experimental import pallas as pl
from jax.experimental.pallas import tpu as pltpu
from jax.sharding import PartitionSpec as P

THRESHOLD = 1.5
RIDGE = 8.0
RANK = 64
PIECE = 128
F32 = jnp.float32
BF16 = jnp.bfloat16
AXES = ("chan", "tm")
MIB = 1 << 20


def exact(first, second, dims):
    return lax.dot_general(
        first,
        second,
        (dims, ((), ())),
        precision=lax.Precision.HIGHEST,
        preferred_element_type=F32,
    )


def single(first, second, dims):
    return lax.dot_general(first, second, (dims, ((), ())), preferred_element_type=F32)


def low_lanes(shape):
    return lax.broadcasted_iota(jnp.int32, shape, 1) < RANK


def two_parts(values):
    high = values.astype(BF16)
    return high, (values - high.astype(F32)).astype(BF16)


def row_stack(packed):
    low = low_lanes(packed.shape)
    high = packed.astype(BF16).astype(F32)
    rest = packed - high
    first = jnp.where(low, high, pltpu.roll(rest, RANK, 1))
    second = jnp.where(low, pltpu.roll(high, RANK, 1), rest)
    return jnp.concatenate([first, second], axis=0).astype(BF16)


def pack_gram(gram):
    return jnp.concatenate([gram[:32], gram[32:]], axis=1)


def inverse(packed):
    flat = jnp.concatenate([packed, pltpu.roll(packed, RANK, 1)], axis=0)
    row = lax.broadcasted_iota(jnp.int32, (RANK, 2 * RANK), 0)
    lane = lax.broadcasted_iota(jnp.int32, (RANK, 2 * RANK), 1)
    flat = jnp.where(lane < RANK, flat, 0.0)
    flat = flat + jnp.where(lane == row, RIDGE, 0.0)
    flat = flat + jnp.where(lane == row + RANK, 1.0, 0.0)
    blocks = [flat[8 * b : 8 * b + 8] for b in range(8)]
    sub = lax.broadcasted_iota(jnp.int32, (8, 2 * RANK), 0)
    for k in range(RANK):
        b, s = divmod(k, 8)
        pivot_row = jnp.broadcast_to(blocks[b][s : s + 1], (8, 2 * RANK))
        pivot = jnp.broadcast_to(pivot_row[:, k : k + 1], (8, 2 * RANK))
        scaled = pivot_row / pivot
        for i in range(8):
            column = jnp.broadcast_to(blocks[i][:, k : k + 1], (8, 2 * RANK))
            changed = blocks[i] - column * scaled
            if i == b:
                changed = jnp.where(sub == s, scaled, changed)
            blocks[i] = changed
    return jnp.concatenate(blocks, axis=0)


def prep_kernel(chan_ref, time_ref, copies_ref, time_out):
    rows = chan_ref[...]
    packed = jnp.concatenate([rows[:RANK], rows[RANK:]], axis=1)
    for i in range(16):
        copies_ref[i] = packed
    time_out[...] = time_ref[...].T


def right_kernel(start, place_ref, *refs):
    if start:
        sources = refs[:4]
        wide_ref, tall_ref, gram_ref, held = refs[4:]
    else:
        mine_ref, other_ref, inv_ref = refs[:3]
        wide_ref, tall_ref, gram_ref, held = refs[3:]
    y, core = place_ref[0], place_ref[1]
    for k in range(4):
        spot = lax.rem(y + 4 - k, 4) if start else k
        if start:
            own, other = sources[k][:RANK], sources[k][RANK:]
        else:
            own, other = mine_ref[RANK * k : RANK * (k + 1)], other_ref[RANK * k : RANK * (k + 1)]
        held[2 * spot + core] = own
        held[2 * spot + 1 - core] = other
    full = jnp.concatenate([held[c] for c in range(8)], axis=1)
    if not start:
        full = exact(inv_ref[:RANK, :RANK], full, ((1,), (0,)))
    gram_ref[...] = pack_gram(exact(full, full, ((1,), (1,))))
    high, low = two_parts(full)
    wide_ref[0:64] = high
    wide_ref[64:128] = high
    wide_ref[128:192] = low
    wide_ref[192:256] = low
    tall_ref[0:64] = high
    tall_ref[64:128] = low


def piece_of(core, q, i):
    return jnp.where(core == 0, 4 * q + i, 4 * i + q)


def rows_kernel(start, j, place_ref, a_ref, left_ref, wide_ref, tall_ref, gram_ref, s_ref, h_ref, l_ref):
    core, u = place_ref[1], place_ref[2]
    q = lax.rem(u + j + 1, 4)
    low = low_lanes((RANK, PIECE))
    for half in range(2):
        spots = []
        stacks = []
        for i in (2 * half, 2 * half + 1):
            p = piece_of(core, q, i)
            spots.append(pl.multiple_of(p * PIECE, PIECE))
            packed = left_ref[p] if start else left_ref[RANK * i : RANK * (i + 1)]
            stacks.append(row_stack(packed))
        stack = jnp.concatenate(stacks, axis=0)
        stack = jnp.concatenate([stack, stack], axis=1)
        total = jnp.zeros((256, PIECE), F32)
        for t in range(4):
            cols = slice(256 * t, 256 * t + 256)
            product = single(stack, wide_ref[:, cols], ((1,), (0,)))
            values = jnp.concatenate([a_ref[pl.ds(s, PIECE), cols] for s in spots], axis=0)
            cleaned = product + jnp.clip(values - product, -THRESHOLD, THRESHOLD)
            high, rest = two_parts(cleaned)
            for n in range(2):
                i = 2 * half + n
                for part, ref in ((high, h_ref), (rest, l_ref)):
                    ref[64 * i : 64 * i + 64, cols] = part[128 * n : 128 * n + 64]
                    ref[256 + 64 * i : 320 + 64 * i, cols] = part[128 * n + 64 : 128 * n + 128]
            total += single(high, tall_ref[:, cols], ((1,), (1,)))
            total += single(rest, tall_ref[:, cols], ((1,), (1,)))
        total = total + pltpu.roll(total, RANK, 1)
        for n in range(2):
            i = 2 * half + n
            s_ref[64 * i : 64 * i + 64] = jnp.where(low, total[128 * n : 128 * n + 64], total[128 * n + 64 : 128 * n + 128])
    s_ref[256:288] = gram_ref[...]


def inverse_kernel(sum_ref, inv_ref):
    found = inverse(sum_ref[256:288])
    low = low_lanes((RANK, PIECE))
    inv_ref[0:64] = jnp.where(low, pltpu.roll(found, RANK, 1), 0.0)
    inv_ref[64:128] = jnp.where(low, 0.0, found)


def cols_kernel(count, has_acc, last, place_ref, inv_ref, *refs):
    s_refs, h_refs, l_refs = refs[:count], refs[count : 2 * count], refs[2 * count : 3 * count]
    refs = refs[3 * count :]
    if has_acc:
        acc_ref, acc_gram_ref = refs[:2]
        refs = refs[2:]
        mine_ref, other_ref = refs[:2]
    else:
        t_ref, gram_ref = refs[:2]
    left_refs = refs[2:]
    core, v = place_ref[1], place_ref[3]
    inv = inv_ref[...]
    gram = acc_gram_ref[...] if has_acc else jnp.zeros((RANK, RANK), F32)
    stacks = []
    for k in range(count):
        packed = exact(s_refs[k][0:256], inv, ((1,), (0,)))
        if not last:
            left_refs[k][...] = packed
        elif not has_acc:
            held = left_refs[1]
            held[...] = packed
            own = held[pl.ds(pl.multiple_of(v * RANK, RANK), RANK)]
            left_refs[0][...] = jnp.concatenate([own[:, :RANK], own[:, RANK:]], axis=0)
        turned = packed.T
        turned = jnp.concatenate([turned[:RANK], turned[RANK:]], axis=1)
        gram += exact(turned, turned, ((1,), (1,)))
        high, rest = two_parts(turned)
        stacks.append(jnp.concatenate([high, rest], axis=0))
    tiles = []
    for t in range(4):
        cols = slice(256 * t, 256 * t + 256)
        total = jnp.zeros((PIECE, 256), F32)
        for k in range(count):
            total += single(stacks[k], h_refs[k][:, cols], ((1,), (0,)))
            total += single(stacks[k], l_refs[k][:, cols], ((1,), (0,)))
        part = total[:RANK] + total[RANK:]
        if has_acc:
            part += acc_ref[:, cols]
            even, odd = part[:, :PIECE], part[:, PIECE:]
            mine_ref[RANK * t : RANK * (t + 1)] = jnp.where(core == 0, even, odd)
            other_ref[RANK * t : RANK * (t + 1)] = jnp.where(core == 0, odd, even)
        else:
            t_ref[:, cols] = part
    if has_acc:
        mine_ref[256:288] = pack_gram(gram)
        other_ref[256:288] = pack_gram(gram)
    else:
        gram_ref[...] = gram


def message_kernel(place_ref, first_ref, second_ref, *out_refs):
    y = place_ref[0]
    gram = first_ref[256:288] + second_ref[256:288]
    for k in range(4):
        rows = pl.ds(pl.multiple_of(lax.rem(y + k, 4) * RANK, RANK), RANK)
        out_refs[k][0:64] = first_ref[rows] + second_ref[rows]
        out_refs[k][64:96] = gram


def final_kernel(m0, m1, m2, m3, out_ref):
    total = m0[...] + m1[...] + m2[...] + m3[...]
    found = inverse(total[64:96])[:, RANK:]
    out_ref[...] = exact(found, total[:64], ((1,), (0,))).T


def outlier_kernel(spots_ref, left_ref, wide_ref, a_ref, out_ref):
    g = pl.program_id(0)
    stack = row_stack(left_ref[pl.ds(pl.multiple_of(g * RANK, RANK), RANK)])
    stack = jnp.concatenate([stack, stack], axis=1)
    for t in range(4):
        cols = slice(256 * t, 256 * t + 256)
        residue = a_ref[:, cols] - single(stack, wide_ref[:, cols], ((1,), (0,)))
        out_ref[:, cols] = residue - jnp.clip(residue, -THRESHOLD, THRESHOLD)


VM = pl.BlockSpec(memory_space=pltpu.VMEM)
SM = pl.BlockSpec(memory_space=pltpu.SMEM)


def shape(*dims, dtype=F32):
    return jax.ShapeDtypeStruct(dims, dtype)


def call(kernel, outs, args, scratch=(), name=None, flops=0, limit=16):
    return pl.pallas_call(
        kernel,
        out_shape=outs,
        in_specs=[SM if a.dtype == jnp.int32 else VM for a in args],
        out_specs=[VM for _ in outs],
        scratch_shapes=list(scratch),
        compiler_params=pltpu.CompilerParams(vmem_limit_bytes=limit * MIB),
        cost_estimate=pl.CostEstimate(flops=flops, bytes_accessed=MIB, transcendentals=0),
        name=name,
    )(*args)


def ring(kind, k):
    pairs = []
    for chan in range(8):
        for tm in range(16):
            y, core = divmod(chan, 2)
            x, z = divmod(tm, 4)
            axis = kind
            if kind == "u":
                axis = "xz"[core]
            elif kind == "v":
                axis = "zx"[core]
            if axis == "x":
                x = (x + k) % 4
            elif axis == "z":
                z = (z + k) % 4
            elif axis == "y":
                y = (y + k) % 4
            else:
                core = 1 - core
            pairs.append((chan * 16 + tm, (2 * y + core) * 16 + 4 * x + z))
    return pairs


def send(values, kind, k=1):
    return lax.ppermute(values, AXES, ring(kind, k))


def sum_around(values, kind):
    return values + send(values, kind, 1) + send(values, kind, 2) + send(values, kind, 3)


def shards(readings, channel_start, time_start):
    chan, tm = lax.axis_index("chan"), lax.axis_index("tm")
    y, core, x, z = chan // 2, chan % 2, tm // 4, tm % 4
    u, v = jnp.where(core == 0, x, z), jnp.where(core == 0, z, x)
    place = jnp.stack([y, core, u, v]).astype(jnp.int32)
    values = readings

    copies, time_piece = call(prep_kernel, [shape(16, 64, 128), shape(64, 128)], [channel_start, time_start], name="prep")
    pair = jnp.concatenate([time_piece, send(time_piece, "core")], axis=0)
    around = [pair] + [send(pair, "y", k) for k in (1, 2, 3)]
    lefts = lax.all_to_all(copies, "tm", split_axis=0, concat_axis=0, tiled=True)
    lefts = [lefts] * 4

    right_args = around
    for sweep in range(2):
        start, last = sweep == 0, sweep == 1
        wide, tall, gram = call(
            functools.partial(right_kernel, start),
            [shape(256, 1024, dtype=BF16), shape(128, 1024, dtype=BF16), shape(32, 128)],
            [place] + list(right_args),
            scratch=[pltpu.VMEM((8, 64, 128), F32)],
            name="right",
        )
        sums, highs, rests = [], [], []
        for j in range(4):
            s, h, r = call(
                functools.partial(rows_kernel, start, j),
                [shape(288, 128), shape(512, 1024, dtype=BF16), shape(512, 1024, dtype=BF16)],
                [place, values, lefts[3 - j], wide, tall, gram],
                name="rows",
                flops=2 * 512 * 1024 * 768,
            )
            sums.append(s)
            highs.append(h)
            rests.append(r)
        got = [send(sums[k - 1], "u", k) for k in (1, 2, 3)]
        own = sums[3] + got[0] + got[1] + got[2]
        own = sum_around(own, "v")
        (inv,) = call(inverse_kernel, [shape(128, 128)], [own], name="inverse", flops=10**9)
        quarters = [own] + [send(own, "u", k) for k in (1, 2, 3)]
        if last:
            left_all = jnp.concatenate(lefts, axis=0)
        first_outs = [shape(64, 1024), shape(64, 64)]
        first_scratch = []
        if last:
            first_outs.append(shape(128, 64))
            first_scratch.append(pltpu.VMEM((256, 128), F32))
        else:
            first_outs.append(shape(256, 128))
        acc, acc_gram, first_left = call(
            functools.partial(cols_kernel, 1, False, last),
            first_outs,
            [place, inv, own, highs[3], rests[3]],
            scratch=first_scratch,
            name="cols_own",
            flops=2 * 512 * 1024 * 256,
        )
        order = (2, 1, 0)
        outs = [shape(288, 128), shape(288, 128)] + ([] if last else [shape(256, 128)] * 3)
        mine, other, *more = call(
            functools.partial(cols_kernel, 3, True, last),
            outs,
            [place, inv] + quarters[1:] + [highs[i] for i in order] + [rests[i] for i in order] + [acc, acc_gram],
            name="cols_rest",
            flops=2 * 1536 * 1024 * 256,
        )
        swapped = send(other, "core")
        if not last:
            half = sum_around(mine + swapped, "y")
            (inv,) = call(inverse_kernel, [shape(128, 128)], [half], name="inverse", flops=10**9)
            right_args = [half, send(half, "core"), inv]
            lefts = [first_left] + list(more)
    messages = call(message_kernel, [shape(96, 128)] * 4, [place, mine, swapped], name="messages")
    parts = [messages[0]] + [send(messages[k], "y", k) for k in (1, 2, 3)]
    (time_out,) = call(final_kernel, [shape(128, 64)], parts, name="final")

    q = jnp.stack([(u + 4 - g // 4) % 4 for g in range(16)])
    i = jnp.arange(16) % 4
    spots = jnp.where(core == 0, 4 * q + i, 4 * i + q).astype(jnp.int32)
    outliers = pl.pallas_call(
        outlier_kernel,
        out_shape=shape(2048, 1024),
        grid_spec=pltpu.PrefetchScalarGridSpec(
            num_scalar_prefetch=1,
            grid=(16,),
            in_specs=[
                pl.BlockSpec((1024, 128), lambda g, spots: (0, 0)),
                pl.BlockSpec((256, 1024), lambda g, spots: (0, 0)),
                pl.BlockSpec((128, 1024), lambda g, spots: (spots[g], 0)),
            ],
            out_specs=pl.BlockSpec((128, 1024), lambda g, spots: (spots[g], 0)),
        ),
        compiler_params=pltpu.CompilerParams(vmem_limit_bytes=16 * MIB),
        cost_estimate=pl.CostEstimate(flops=2 * 2048 * 1024 * 256, bytes_accessed=16 * MIB, transcendentals=0),
        name="outliers",
    )(spots, left_all, wide, readings)
    return outliers, first_left, time_out


def solution(mesh):
    in_specs = (P("chan", "tm"), P(("chan", "tm"), None), P(("tm", "chan"), None))
    out_specs = (P("chan", "tm"), P(("chan", "tm"), None), P(("tm", "chan"), None))
    return jax.shard_map(shards, mesh=mesh, in_specs=in_specs, out_specs=out_specs, check_vma=False)
```

```python
import functools

import jax
import jax.numpy as jnp
import numpy as np
from jax import lax
from jax.experimental import pallas as pl
from jax.experimental.pallas import tpu as pltpu
from jax.sharding import PartitionSpec as P

THRESHOLD = 1.5
RIDGE = 8.0
RANK = 64
PIECE = 128
F32 = jnp.float32
BF16 = jnp.bfloat16
AXES = ("chan", "tm")
MIB = 1 << 20


def exact(first, second, dims):
    return lax.dot_general(
        first,
        second,
        (dims, ((), ())),
        precision=lax.Precision.HIGHEST,
        preferred_element_type=F32,
    )


def single(first, second, dims):
    return lax.dot_general(first, second, (dims, ((), ())), preferred_element_type=F32)


def low_lanes(shape):
    return lax.broadcasted_iota(jnp.int32, shape, 1) < RANK


def two_parts(values):
    high = values.astype(BF16)
    return high, (values - high.astype(F32)).astype(BF16)


def row_stack(packed):
    low = low_lanes(packed.shape)
    high = packed.astype(BF16).astype(F32)
    rest = packed - high
    first = jnp.where(low, high, pltpu.roll(rest, RANK, 1))
    second = jnp.where(low, pltpu.roll(high, RANK, 1), rest)
    return jnp.concatenate([first, second], axis=0).astype(BF16)


def pack_gram(gram):
    return jnp.concatenate([gram[:32], gram[32:]], axis=1)


def solve_rows(rows, e):
    n = len(rows)
    for t in range(0, n, 2):
        a, b, c, d = e[t][t], e[t][t + 1], e[t + 1][t], e[t + 1][t + 1]
        scale = 1.0 / (a * d - b * c)
        a, b, c, d = a * scale, b * scale, c * scale, d * scale
        rows[t], rows[t + 1] = d * rows[t] - b * rows[t + 1], a * rows[t + 1] - c * rows[t]
        for j in range(t + 2, n):
            e[t][j], e[t + 1][j] = d * e[t][j] - b * e[t + 1][j], a * e[t + 1][j] - c * e[t][j]
        for i in range(n):
            if i in (t, t + 1):
                continue
            f, g = e[i][t], e[i][t + 1]
            rows[i] = rows[i] - (f * rows[t] + g * rows[t + 1])
            for j in range(t + 2, n):
                e[i][j] = e[i][j] - (f * e[t][j] + g * e[t + 1][j])
    return rows


def inverse(packed):
    flat = jnp.concatenate([packed, pltpu.roll(packed, RANK, 1)], axis=0)
    row = lax.broadcasted_iota(jnp.int32, (RANK, 2 * RANK), 0)
    lane = lax.broadcasted_iota(jnp.int32, (RANK, 2 * RANK), 1)
    flat = jnp.where(lane < RANK, flat, 0.0)
    flat = flat + jnp.where(lane == row, RIDGE, 0.0)
    flat = flat + jnp.where(lane == row + RANK, 1.0, 0.0)
    full = (8, 2 * RANK)
    blocks = [flat[8 * b : 8 * b + 8] for b in range(8)]
    sub = lax.broadcasted_iota(jnp.int32, full, 0)
    for b in range(8):
        k = 8 * b
        rows = [jnp.broadcast_to(blocks[b][i : i + 1], full) for i in range(8)]
        entries = [[jnp.broadcast_to(r[:, k + j : k + j + 1], full) for j in range(8)] for r in rows]
        rows = solve_rows(rows, entries)
        for i in range(8):
            changed = blocks[i]
            for j in range(8):
                if i == b:
                    changed = jnp.where(sub == j, rows[j], changed)
                else:
                    changed = changed - jnp.broadcast_to(blocks[i][:, k + j : k + j + 1], full) * rows[j]
            blocks[i] = changed
    return jnp.concatenate(blocks, axis=0)


def quarter_kernel(place_ref, *refs):
    v = place_ref[3]
    for k in range(4):
        rows = pl.ds(pl.multiple_of(lax.rem(v + 4 - k, 4) * RANK, RANK), RANK)
        piece = refs[k][...].T
        refs[-1][rows] = jnp.concatenate([piece[:RANK], piece[RANK:]], axis=1)


def right_kernel(start, place_ref, *refs):
    if start:
        owns, others = refs[:4], refs[4:8]
        refs = refs[8:]
    else:
        mine_ref, other_ref, inv_ref = refs[:3]
        refs = refs[3:]
    wide_ref, tall_ref, gram_ref, held = refs
    y, core = place_ref[0], place_ref[1]
    for k in range(4):
        spot = lax.rem(y + 4 - k, 4) if start else k
        if start:
            own, other = owns[k][...], others[k][...]
        else:
            own, other = mine_ref[RANK * k : RANK * (k + 1)], other_ref[RANK * k : RANK * (k + 1)]
        held[2 * spot + core] = own
        held[2 * spot + 1 - core] = other
    full = jnp.concatenate([held[c] for c in range(8)], axis=1)
    if not start:
        full = exact(inv_ref[:RANK, :RANK], full, ((1,), (0,)))
    gram_ref[...] = pack_gram(exact(full, full, ((1,), (1,))))
    high, low = two_parts(full)
    wide_ref[0:64] = high
    wide_ref[64:128] = high
    wide_ref[128:192] = low
    wide_ref[192:256] = low
    tall_ref[0:64] = high
    tall_ref[64:128] = low


def piece_of(core, q, i):
    return jnp.where(core == 0, 4 * q + i, 4 * i + q)


def rows_kernel(j, place_ref, a_ref, left_ref, wide_ref, tall_ref, gram_ref, s_ref, h_ref, l_ref):
    core, u = place_ref[1], place_ref[2]
    q = lax.rem(u + j + 1, 4)
    low = low_lanes((RANK, PIECE))
    for half in range(2):
        spots = []
        stacks = []
        for i in (2 * half, 2 * half + 1):
            p = piece_of(core, q, i)
            spots.append(pl.multiple_of(p * PIECE, PIECE))
            packed = left_ref[RANK * i : RANK * (i + 1)]
            stacks.append(row_stack(packed))
        stack = jnp.concatenate(stacks, axis=0)
        stack = jnp.concatenate([stack, stack], axis=1)
        product = single(stack, wide_ref[...], ((1,), (0,)))
        values = jnp.concatenate([a_ref[pl.ds(s, PIECE)] for s in spots], axis=0)
        cleaned = product + jnp.clip(values - product, -THRESHOLD, THRESHOLD)
        high, rest = two_parts(cleaned)
        for n in range(2):
            i = 2 * half + n
            for part, ref in ((high, h_ref), (rest, l_ref)):
                ref[64 * i : 64 * i + 64] = part[128 * n : 128 * n + 64]
                ref[256 + 64 * i : 320 + 64 * i] = part[128 * n + 64 : 128 * n + 128]
        total = single(high, tall_ref[...], ((1,), (1,))) + single(rest, tall_ref[...], ((1,), (1,)))
        total = total + pltpu.roll(total, RANK, 1)
        for n in range(2):
            i = 2 * half + n
            s_ref[64 * i : 64 * i + 64] = jnp.where(low, total[128 * n : 128 * n + 64], total[128 * n + 64 : 128 * n + 128])
    s_ref[256:288] = gram_ref[...]


def inverse_kernel(sum_ref, inv_ref):
    found = inverse(sum_ref[...])
    low = low_lanes((RANK, PIECE))
    inv_ref[0:64] = jnp.where(low, pltpu.roll(found, RANK, 1), 0.0)
    inv_ref[64:128] = jnp.where(low, 0.0, found)


def cols_kernel(count, has_acc, last, place_ref, inv_ref, *refs):
    s_refs, h_refs, l_refs = refs[:count], refs[count : 2 * count], refs[2 * count : 3 * count]
    refs = refs[3 * count :]
    if has_acc:
        acc_ref, acc_gram_ref = refs[:2]
        refs = refs[2:]
        mine_ref, other_ref = refs[:2]
    else:
        t_ref, gram_ref = refs[:2]
    left_refs = refs[2:]
    core, v = place_ref[1], place_ref[3]
    inv = inv_ref[...]
    gram = acc_gram_ref[...] if has_acc else jnp.zeros((RANK, RANK), F32)
    stacks = []
    for k in range(count):
        packed = exact(s_refs[k][0:256], inv, ((1,), (0,)))
        if not last:
            left_refs[k][...] = packed
        elif not has_acc:
            held = left_refs[1]
            held[...] = packed
            own = held[pl.ds(pl.multiple_of(v * RANK, RANK), RANK)]
            left_refs[0][...] = jnp.concatenate([own[:, :RANK], own[:, RANK:]], axis=0).T
        turned = packed.T
        turned = jnp.concatenate([turned[:RANK], turned[RANK:]], axis=1)
        gram += exact(turned, turned, ((1,), (1,)))
        high, rest = two_parts(turned)
        stacks.append(jnp.concatenate([high, rest], axis=0))
    tiles = []
    for t in range(4):
        cols = slice(256 * t, 256 * t + 256)
        total = jnp.zeros((PIECE, 256), F32)
        for k in range(count):
            total += single(stacks[k], h_refs[k][:, cols], ((1,), (0,)))
            total += single(stacks[k], l_refs[k][:, cols], ((1,), (0,)))
        part = total[:RANK] + total[RANK:]
        if has_acc:
            part += acc_ref[:, cols]
            even, odd = part[:, :PIECE], part[:, PIECE:]
            mine_ref[RANK * t : RANK * (t + 1)] = jnp.where(core == 0, even, odd)
            other_ref[RANK * t : RANK * (t + 1)] = jnp.where(core == 0, odd, even)
        else:
            t_ref[:, cols] = part
    if has_acc:
        mine_ref[256:288] = pack_gram(gram)
        other_ref[256:288] = pack_gram(gram)
    else:
        gram_ref[...] = gram


def message_kernel(place_ref, first_ref, second_ref, *out_refs):
    y = place_ref[0]
    gram = first_ref[256:288] + second_ref[256:288]
    for k in range(4):
        rows = pl.ds(pl.multiple_of(lax.rem(y + k, 4) * RANK, RANK), RANK)
        out_refs[k][0:64] = first_ref[rows] + second_ref[rows]
        out_refs[k][64:96] = gram


def final_kernel(m0, m1, m2, m3, out_ref):
    total = m0[...] + m1[...] + m2[...] + m3[...]
    found = inverse(total[64:96])[:, RANK:]
    out_ref[...] = exact(found, total[:64], ((1,), (0,)))


def outlier_kernel(spots_ref, left_ref, wide_ref, a_ref, after_ref, out_ref, token_ref):
    g = pl.program_id(0)
    stacks = []
    for n in range(2):
        spot = pl.multiple_of(spots_ref[4 + 2 * g + n] * RANK, RANK)
        stacks.append(row_stack(left_ref[pl.ds(spot, RANK)]))
    stack = jnp.concatenate(stacks, axis=0)
    stack = jnp.concatenate([stack, stack], axis=1)
    rows = pl.ds(pl.multiple_of(g * 256, 256), 256)
    for t in range(2):
        cols = slice(512 * t, 512 * t + 512)
        residue = a_ref[rows, cols] - single(stack, wide_ref[:, cols], ((1,), (0,)))
        out_ref[:, cols] = residue - jnp.clip(residue, -THRESHOLD, THRESHOLD)
    token_ref[...] = jnp.zeros_like(token_ref)


def sum_kernel(count, *refs):
    total = refs[0][...]
    for ref in refs[1:count]:
        total = total + ref[...]
    refs[-2][...] = total[:256]
    refs[-1][...] = total[256:]


VM = pl.BlockSpec(memory_space=pltpu.VMEM)
SM = pl.BlockSpec(memory_space=pltpu.SMEM)
ANY = pl.BlockSpec(memory_space=pl.ANY)


def shape(*dims, dtype=F32):
    return jax.ShapeDtypeStruct(dims, dtype)


def call(kernel, outs, args, scratch=(), name=None, flops=0, limit=16):
    return pl.pallas_call(
        kernel,
        out_shape=outs,
        in_specs=[SM if a.dtype == jnp.int32 else VM for a in args],
        out_specs=[VM for _ in outs],
        scratch_shapes=list(scratch),
        compiler_params=pltpu.CompilerParams(vmem_limit_bytes=limit * MIB),
        cost_estimate=pl.CostEstimate(flops=flops, bytes_accessed=MIB, transcendentals=0),
        name=name,
    )(*args)


def ring(kind, k):
    pairs = []
    for chan in range(8):
        for tm in range(16):
            y, core = divmod(chan, 2)
            x, z = divmod(tm, 4)
            axis = kind
            if kind == "u":
                axis = "xz"[core]
            elif kind == "v":
                axis = "zx"[core]
            if axis == "x":
                x = (x + k) % 4
            elif axis == "z":
                z = (z + k) % 4
            elif axis == "y":
                y = (y + k) % 4
            else:
                core = 1 - core
            pairs.append((chan * 16 + tm, (2 * y + core) * 16 + 4 * x + z))
    return pairs


def send(values, kind, k=1):
    return lax.ppermute(values, AXES, ring(kind, k))


def places():
    table = np.zeros((128, 20), np.int32)
    for chan in range(8):
        for tm in range(16):
            y, core = divmod(chan, 2)
            x, z = divmod(tm, 4)
            u, v = (x, z) if core == 0 else (z, x)
            spots = []
            for p in range(16):
                q, i = divmod(p, 4)
                if core == 1:
                    q, i = i, q
                spots.append((u - q) % 4 * 4 + i)
            table[chan * 16 + tm] = [y, core, u, v] + spots
    return table


def shards(readings, channel_start, time_start):
    chan, tm = lax.axis_index("chan"), lax.axis_index("tm")
    place = lax.dynamic_index_in_dim(jnp.asarray(places()), chan * 16 + tm, keepdims=False)

    chan_piece, time_piece = channel_start.T, time_start.T
    lefts = [chan_piece] + [send(chan_piece, "v", k) for k in (1, 2, 3)]
    owns = [time_piece] + [send(time_piece, "y", k) for k in (1, 2, 3)]
    (left_own,) = call(quarter_kernel, [shape(256, 128)], [place] + lefts + owns[1:], name="quarter", flops=5 * 10**9)
    lefts = [left_own] + [send(left_own, "u", k) for k in (1, 2, 3)]
    others = [send(piece, "core") for piece in owns]
    right_args = owns + others
    for sweep in range(2):
        start, last = sweep == 0, sweep == 1
        wide, tall, gram = call(
            functools.partial(right_kernel, start),
            [shape(256, 1024, dtype=BF16), shape(128, 1024, dtype=BF16), shape(32, 128)],
            [place] + list(right_args),
            scratch=[pltpu.VMEM((8, 64, 128), F32)],
            name="right",
            flops=5 * 10**9,
        )
        sums, highs, rests = [], [], []
        for j in range(4):
            s, h, r = call(
                functools.partial(rows_kernel, j),
                [shape(288, 128), pltpu.VMEM((512, 1024), BF16), pltpu.VMEM((512, 1024), BF16)],
                [place, readings, lefts[3 - j], wide, tall, gram],
                name="rows",
                flops=2 * 512 * 1024 * 768,
            )
            sums.append(s)
            highs.append(h)
            rests.append(r)
        got = [send(sums[k - 1], "u", k) for k in (1, 2, 3)]
        own = sums[3] + got[0] + got[1] + got[2]
        if last:
            outliers, token = pl.pallas_call(
                outlier_kernel,
                out_shape=[shape(2048, 1024), shape(8, 128)],
                grid_spec=pltpu.PrefetchScalarGridSpec(
                    num_scalar_prefetch=1,
                    grid=(8,),
                    in_specs=[
                        pl.BlockSpec((1024, 128), lambda g, spots: (0, 0)),
                        pl.BlockSpec((256, 1024), lambda g, spots: (0, 0)),
                        VM,
                        ANY,
                    ],
                    out_specs=[
                        pl.BlockSpec((256, 1024), lambda g, spots: (g, 0)),
                        pl.BlockSpec((8, 128), lambda g, spots: (0, 0)),
                    ],
                ),
                compiler_params=pltpu.CompilerParams(vmem_limit_bytes=12 * MIB),
                cost_estimate=pl.CostEstimate(flops=2 * 2048 * 1024 * 256, bytes_accessed=16 * MIB, transcendentals=0),
                name="outliers",
            )(place, jnp.concatenate(lefts, axis=0), wide, readings, own)
        parts = [own] + [send(own, "v", k) for k in (1, 2, 3)]
        own, gram = call(functools.partial(sum_kernel, 4), [shape(256, 128), shape(32, 128)], parts + ([token] if last else []), name="sum")
        (inv,) = call(inverse_kernel, [shape(128, 128)], [gram], name="inverse", flops=10**9)
        quarters = [own] + [send(own, "u", k) for k in (1, 2, 3)]
        first_outs = [shape(64, 1024), shape(64, 64)]
        first_scratch = []
        if last:
            first_outs.append(shape(64, 128))
            first_scratch.append(pltpu.VMEM((256, 128), F32))
        else:
            first_outs.append(shape(256, 128))
        acc, acc_gram, first_left = call(
            functools.partial(cols_kernel, 1, False, last),
            first_outs,
            [place, inv, own, highs[3], rests[3]],
            scratch=first_scratch,
            name="cols_own",
            flops=2 * 512 * 1024 * 256,
        )
        order = (2, 1, 0)
        outs = [shape(288, 128), shape(288, 128)] + ([] if last else [shape(256, 128)] * 3)
        mine, other, *more = call(
            functools.partial(cols_kernel, 3, True, last),
            outs,
            [place, inv] + quarters[1:] + [highs[i] for i in order] + [rests[i] for i in order] + [acc, acc_gram],
            name="cols_rest",
            flops=2 * 1536 * 1024 * 256,
        )
        swapped = send(other, "core")
        if not last:
            half = mine + swapped
            parts = [half] + [send(half, "y", k) for k in (1, 2, 3)]
            half, gram = call(functools.partial(sum_kernel, 4), [shape(256, 128), shape(32, 128)], parts, name="sum")
            (inv,) = call(inverse_kernel, [shape(128, 128)], [gram], name="inverse", flops=10**9)
            right_args = [half, send(half, "core"), inv]
            lefts = [first_left] + list(more)
    messages = call(message_kernel, [shape(96, 128)] * 4, [place, mine, swapped], name="messages")
    parts = [messages[0]] + [send(messages[k], "y", k) for k in (1, 2, 3)]
    (time_out,) = call(final_kernel, [shape(64, 128)], parts, name="final")

    return outliers, first_left.T, time_out.T


def solution(mesh):
    in_specs = (P("chan", "tm"), P(("chan", "tm"), None), P(("tm", "chan"), None))
    out_specs = (P("chan", "tm"), P(("chan", "tm"), None), P(("tm", "chan"), None))
    return jax.shard_map(shards, mesh=mesh, in_specs=in_specs, out_specs=out_specs, check_vma=False)
```

```python
import functools

import jax
import jax.numpy as jnp
import numpy as np
from jax import lax
from jax.experimental import pallas as pl
from jax.experimental.pallas import tpu as pltpu
from jax.sharding import PartitionSpec as P

THRESHOLD = 1.5
RIDGE = 8.0
RANK = 64
PIECE = 128
F32 = jnp.float32
BF16 = jnp.bfloat16
AXES = ("chan", "tm")
MIB = 1 << 20


def exact(first, second, dims):
    return lax.dot_general(
        first,
        second,
        (dims, ((), ())),
        precision=lax.Precision.HIGHEST,
        preferred_element_type=F32,
    )


def single(first, second, dims):
    return lax.dot_general(first, second, (dims, ((), ())), preferred_element_type=F32)


def low_lanes(shape):
    return lax.broadcasted_iota(jnp.int32, shape, 1) < RANK


def two_parts(values):
    high = values.astype(BF16)
    return high, (values - high.astype(F32)).astype(BF16)


def row_stack(packed):
    low = low_lanes(packed.shape)
    high = packed.astype(BF16).astype(F32)
    rest = packed - high
    first = jnp.where(low, high, pltpu.roll(rest, RANK, 1))
    second = jnp.where(low, pltpu.roll(high, RANK, 1), rest)
    return jnp.concatenate([first, second], axis=0).astype(BF16)


def gram_of(stack):
    four = single(stack, stack, ((1,), (1,)))
    two = four[:RANK] + four[RANK:]
    return two[:, :RANK] + two[:, RANK:]


def pack_gram(gram):
    return jnp.concatenate([gram[:32], gram[32:]], axis=1)


def solve_rows(rows, e):
    n = len(rows)
    for t in range(0, n, 2):
        a, b, c, d = e[t][t], e[t][t + 1], e[t + 1][t], e[t + 1][t + 1]
        scale = 1.0 / (a * d - b * c)
        a, b, c, d = a * scale, b * scale, c * scale, d * scale
        rows[t], rows[t + 1] = d * rows[t] - b * rows[t + 1], a * rows[t + 1] - c * rows[t]
        for j in range(t + 2, n):
            e[t][j], e[t + 1][j] = d * e[t][j] - b * e[t + 1][j], a * e[t + 1][j] - c * e[t][j]
        for i in range(n):
            if i in (t, t + 1):
                continue
            f, g = e[i][t], e[i][t + 1]
            rows[i] = rows[i] - (f * rows[t] + g * rows[t + 1])
            for j in range(t + 2, n):
                e[i][j] = e[i][j] - (f * e[t][j] + g * e[t + 1][j])
    return rows


def inverse(packed):
    flat = jnp.concatenate([packed, pltpu.roll(packed, RANK, 1)], axis=0)
    row = lax.broadcasted_iota(jnp.int32, (RANK, 2 * RANK), 0)
    lane = lax.broadcasted_iota(jnp.int32, (RANK, 2 * RANK), 1)
    flat = jnp.where(lane < RANK, flat, 0.0)
    flat = flat + jnp.where(lane == row, RIDGE, 0.0)
    flat = flat + jnp.where(lane == row + RANK, 1.0, 0.0)
    full = (8, 2 * RANK)
    blocks = [flat[8 * b : 8 * b + 8] for b in range(8)]
    sub = lax.broadcasted_iota(jnp.int32, full, 0)
    for b in range(8):
        k = 8 * b
        rows = [jnp.broadcast_to(blocks[b][i : i + 1], full) for i in range(8)]
        entries = [[jnp.broadcast_to(r[:, k + j : k + j + 1], full) for j in range(8)] for r in rows]
        rows = solve_rows(rows, entries)
        for i in range(8):
            changed = blocks[i]
            for j in range(8):
                if i == b:
                    changed = jnp.where(sub == j, rows[j], changed)
                else:
                    changed = changed - jnp.broadcast_to(blocks[i][:, k + j : k + j + 1], full) * rows[j]
            blocks[i] = changed
    return jnp.concatenate(blocks, axis=0)


def quarter_kernel(place_ref, *refs):
    v = place_ref[3]
    for k in range(4):
        rows = pl.ds(pl.multiple_of((v ^ k) * RANK, RANK), RANK)
        piece = refs[k][...].T
        refs[-1][rows] = jnp.concatenate([piece[:RANK], piece[RANK:]], axis=1)


def right_kernel(start, place_ref, *refs):
    if start:
        owns, others = refs[:4], refs[4:8]
        refs = refs[8:]
    else:
        mine_ref, other_ref, inv_ref = refs[:3]
        refs = refs[3:]
    wide_ref, tall_ref, gram_ref, held = refs
    y, core = place_ref[0], place_ref[1]
    for k in range(4):
        spot = y ^ k if start else k
        if start:
            own, other = owns[k][...], others[k][...]
        else:
            own, other = mine_ref[RANK * k : RANK * (k + 1)], other_ref[RANK * k : RANK * (k + 1)]
        held[2 * spot + core] = own
        held[2 * spot + 1 - core] = other
    full = jnp.concatenate([held[c] for c in range(8)], axis=1)
    if not start:
        full = exact(inv_ref[:RANK, :RANK], full, ((1,), (0,)))
    high, low = two_parts(full)
    gram_ref[...] = pack_gram(gram_of(jnp.concatenate([high, low], axis=0)))
    wide_ref[0:64] = high
    wide_ref[64:128] = high
    wide_ref[128:192] = low
    wide_ref[192:256] = low
    tall_ref[0:64] = high
    tall_ref[64:128] = low


def piece_of(core, q, i):
    return jnp.where(core == 0, 4 * q + i, 4 * i + q)


def rows_kernel(j, place_ref, a_ref, left_ref, wide_ref, tall_ref, gram_ref, s_ref, h_ref, l_ref):
    core, u = place_ref[1], place_ref[2]
    q = u ^ ((j + 1) % 4)
    low = low_lanes((RANK, PIECE))
    for half in range(2):
        spots = []
        stacks = []
        for i in (2 * half, 2 * half + 1):
            p = piece_of(core, q, i)
            spots.append(pl.multiple_of(p * PIECE, PIECE))
            packed = left_ref[RANK * i : RANK * (i + 1)]
            stacks.append(row_stack(packed))
        stack = jnp.concatenate(stacks, axis=0)
        stack = jnp.concatenate([stack, stack], axis=1)
        product = single(stack, wide_ref[...], ((1,), (0,)))
        values = jnp.concatenate([a_ref[pl.ds(s, PIECE)] for s in spots], axis=0)
        cleaned = product + jnp.clip(values - product, -THRESHOLD, THRESHOLD)
        high, rest = two_parts(cleaned)
        for n in range(2):
            i = 2 * half + n
            for part, ref in ((high, h_ref), (rest, l_ref)):
                ref[64 * i : 64 * i + 64] = part[128 * n : 128 * n + 64]
                ref[256 + 64 * i : 320 + 64 * i] = part[128 * n + 64 : 128 * n + 128]
        total = single(high, tall_ref[...], ((1,), (1,))) + single(rest, tall_ref[...], ((1,), (1,)))
        total = total + pltpu.roll(total, RANK, 1)
        for n in range(2):
            i = 2 * half + n
            s_ref[64 * i : 64 * i + 64] = jnp.where(low, total[128 * n : 128 * n + 64], total[128 * n + 64 : 128 * n + 128])
    s_ref[256:288] = gram_ref[...]


def inverse_kernel(sum_ref, inv_ref):
    found = inverse(sum_ref[...])
    low = low_lanes((RANK, PIECE))
    inv_ref[0:64] = jnp.where(low, pltpu.roll(found, RANK, 1), 0.0)
    inv_ref[64:128] = jnp.where(low, 0.0, found)


def cols_kernel(count, has_acc, last, place_ref, inv_ref, *refs):
    s_refs, h_refs, l_refs = refs[:count], refs[count : 2 * count], refs[2 * count : 3 * count]
    refs = refs[3 * count :]
    if has_acc:
        acc_ref, acc_gram_ref = refs[:2]
        refs = refs[2:]
        mine_ref, other_ref = refs[:2]
    else:
        t_ref, gram_ref = refs[:2]
    left_refs = refs[2:]
    core, v = place_ref[1], place_ref[3]
    inv = inv_ref[...]
    gram = acc_gram_ref[...] if has_acc else jnp.zeros((RANK, RANK), F32)
    stacks = []
    for k in range(count):
        packed = exact(s_refs[k][0:256], inv, ((1,), (0,)))
        if not last:
            left_refs[k][...] = packed
        elif not has_acc:
            held = left_refs[1]
            held[...] = packed
            own = held[pl.ds(pl.multiple_of(v * RANK, RANK), RANK)]
            left_refs[0][...] = jnp.concatenate([own[:, :RANK], own[:, RANK:]], axis=0).T
        turned = packed.T
        turned = jnp.concatenate([turned[:RANK], turned[RANK:]], axis=1)
        stack = jnp.concatenate(two_parts(turned), axis=0)
        gram += gram_of(stack)
        stacks.append(stack)
    tiles = []
    for t in range(4):
        cols = slice(256 * t, 256 * t + 256)
        total = jnp.zeros((PIECE, 256), F32)
        for k in range(count):
            total += single(stacks[k], h_refs[k][:, cols], ((1,), (0,)))
            total += single(stacks[k], l_refs[k][:, cols], ((1,), (0,)))
        part = total[:RANK] + total[RANK:]
        if has_acc:
            part += acc_ref[:, cols]
            even, odd = part[:, :PIECE], part[:, PIECE:]
            mine_ref[RANK * t : RANK * (t + 1)] = jnp.where(core == 0, even, odd)
            other_ref[RANK * t : RANK * (t + 1)] = jnp.where(core == 0, odd, even)
        else:
            t_ref[:, cols] = part
    if has_acc:
        mine_ref[256:288] = pack_gram(gram)
        other_ref[256:288] = pack_gram(gram)
    else:
        gram_ref[...] = gram


def message_kernel(place_ref, first_ref, second_ref, *out_refs):
    y = place_ref[0]
    gram = first_ref[256:288] + second_ref[256:288]
    for k in range(4):
        rows = pl.ds(pl.multiple_of((y ^ k) * RANK, RANK), RANK)
        out_refs[k][0:64] = first_ref[rows] + second_ref[rows]
        out_refs[k][64:96] = gram


def final_kernel(m0, m1, m2, m3, out_ref):
    total = m0[...] + m1[...] + m2[...] + m3[...]
    found = inverse(total[64:96])[:, RANK:]
    out_ref[...] = exact(found, total[:64], ((1,), (0,)))


def outlier_kernel(spots_ref, left_ref, wide_ref, a_ref, after_ref, out_ref, token_ref):
    g = pl.program_id(0)
    stacks = []
    for n in range(2):
        spot = pl.multiple_of(spots_ref[4 + 2 * g + n] * RANK, RANK)
        stacks.append(row_stack(left_ref[pl.ds(spot, RANK)]))
    stack = jnp.concatenate(stacks, axis=0)
    stack = jnp.concatenate([stack, stack], axis=1)
    rows = pl.ds(pl.multiple_of(g * 256, 256), 256)
    for t in range(2):
        cols = slice(512 * t, 512 * t + 512)
        residue = a_ref[rows, cols] - single(stack, wide_ref[:, cols], ((1,), (0,)))
        out_ref[:, cols] = residue - jnp.clip(residue, -THRESHOLD, THRESHOLD)
    token_ref[...] = jnp.zeros_like(token_ref)


def sum_kernel(count, *refs):
    total = refs[0][...]
    for ref in refs[1:count]:
        total = total + ref[...]
    refs[-2][...] = total[:256]
    refs[-1][...] = total[256:]


VM = pl.BlockSpec(memory_space=pltpu.VMEM)
SM = pl.BlockSpec(memory_space=pltpu.SMEM)
ANY = pl.BlockSpec(memory_space=pl.ANY)


def shape(*dims, dtype=F32):
    return jax.ShapeDtypeStruct(dims, dtype)


def call(kernel, outs, args, scratch=(), name=None, flops=0, limit=16):
    return pl.pallas_call(
        kernel,
        out_shape=outs,
        in_specs=[SM if a.dtype == jnp.int32 else VM for a in args],
        out_specs=[VM for _ in outs],
        scratch_shapes=list(scratch),
        compiler_params=pltpu.CompilerParams(vmem_limit_bytes=limit * MIB),
        cost_estimate=pl.CostEstimate(flops=flops, bytes_accessed=MIB, transcendentals=0),
        name=name,
    )(*args)


def ring(kind, k):
    pairs = []
    for chan in range(8):
        for tm in range(16):
            y, core = divmod(chan, 2)
            x, z = divmod(tm, 4)
            axis = kind
            if kind == "u":
                axis = "xz"[core]
            elif kind == "v":
                axis = "zx"[core]
            if axis == "x":
                x = x ^ k
            elif axis == "z":
                z = z ^ k
            elif axis == "y":
                y = y ^ k
            else:
                core = 1 - core
            pairs.append((chan * 16 + tm, (2 * y + core) * 16 + 4 * x + z))
    return pairs


def send(values, kind, k=1):
    return lax.ppermute(values, AXES, ring(kind, k))


def places():
    table = np.zeros((128, 20), np.int32)
    for chan in range(8):
        for tm in range(16):
            y, core = divmod(chan, 2)
            x, z = divmod(tm, 4)
            u, v = (x, z) if core == 0 else (z, x)
            spots = []
            for p in range(16):
                q, i = divmod(p, 4)
                if core == 1:
                    q, i = i, q
                spots.append((u ^ q) * 4 + i)
            table[chan * 16 + tm] = [y, core, u, v] + spots
    return table


def shards(readings, channel_start, time_start):
    chan, tm = lax.axis_index("chan"), lax.axis_index("tm")
    place = lax.dynamic_index_in_dim(jnp.asarray(places()), chan * 16 + tm, keepdims=False)

    chan_piece, time_piece = channel_start.T, time_start.T
    lefts = [chan_piece] + [send(chan_piece, "v", k) for k in (1, 2, 3)]
    owns = [time_piece] + [send(time_piece, "y", k) for k in (1, 2, 3)]
    (left_own,) = call(quarter_kernel, [shape(256, 128)], [place] + lefts + owns[1:], name="quarter", flops=5 * 10**9)
    lefts = [left_own] + [send(left_own, "u", k) for k in (1, 2, 3)]
    others = [send(piece, "core") for piece in owns]
    right_args = owns + others
    for sweep in range(2):
        start, last = sweep == 0, sweep == 1
        wide, tall, gram = call(
            functools.partial(right_kernel, start),
            [shape(256, 1024, dtype=BF16), shape(128, 1024, dtype=BF16), shape(32, 128)],
            [place] + list(right_args),
            scratch=[pltpu.VMEM((8, 64, 128), F32)],
            name="right",
            flops=5 * 10**9,
        )
        sums, highs, rests = [], [], []
        for j in range(4):
            s, h, r = call(
                functools.partial(rows_kernel, j),
                [shape(288, 128), pltpu.VMEM((512, 1024), BF16), pltpu.VMEM((512, 1024), BF16)],
                [place, readings, lefts[(j + 1) % 4], wide, tall, gram],
                name="rows",
                flops=2 * 512 * 1024 * 768,
            )
            sums.append(s)
            highs.append(h)
            rests.append(r)
        got = [send(sums[k - 1], "u", k) for k in (1, 2, 3)]
        own = sums[3] + got[0] + got[1] + got[2]
        if last:
            outliers, token = pl.pallas_call(
                outlier_kernel,
                out_shape=[shape(2048, 1024), shape(8, 128)],
                grid_spec=pltpu.PrefetchScalarGridSpec(
                    num_scalar_prefetch=1,
                    grid=(8,),
                    in_specs=[
                        pl.BlockSpec((1024, 128), lambda g, spots: (0, 0)),
                        pl.BlockSpec((256, 1024), lambda g, spots: (0, 0)),
                        VM,
                        ANY,
                    ],
                    out_specs=[
                        pl.BlockSpec((256, 1024), lambda g, spots: (g, 0)),
                        pl.BlockSpec((8, 128), lambda g, spots: (0, 0)),
                    ],
                ),
                compiler_params=pltpu.CompilerParams(vmem_limit_bytes=12 * MIB),
                cost_estimate=pl.CostEstimate(flops=2 * 2048 * 1024 * 256, bytes_accessed=16 * MIB, transcendentals=0),
                name="outliers",
            )(place, jnp.concatenate(lefts, axis=0), wide, readings, own)
        parts = [own] + [send(own, "v", k) for k in (1, 2, 3)]
        own, gram = call(functools.partial(sum_kernel, 4), [shape(256, 128), shape(32, 128)], parts + ([token] if last else []), name="sum")
        (inv,) = call(inverse_kernel, [shape(128, 128)], [gram], name="inverse", flops=10**9)
        quarters = [own] + [send(own, "u", k) for k in (1, 2, 3)]
        first_outs = [shape(64, 1024), shape(64, 64)]
        first_scratch = []
        if last:
            first_outs.append(shape(64, 128))
            first_scratch.append(pltpu.VMEM((256, 128), F32))
        else:
            first_outs.append(shape(256, 128))
        acc, acc_gram, first_left = call(
            functools.partial(cols_kernel, 1, False, last),
            first_outs,
            [place, inv, own, highs[3], rests[3]],
            scratch=first_scratch,
            name="cols_own",
            flops=2 * 512 * 1024 * 256,
        )
        order = (0, 1, 2)
        outs = [shape(288, 128), shape(288, 128)] + ([] if last else [shape(256, 128)] * 3)
        mine, other, *more = call(
            functools.partial(cols_kernel, 3, True, last),
            outs,
            [place, inv] + quarters[1:] + [highs[i] for i in order] + [rests[i] for i in order] + [acc, acc_gram],
            name="cols_rest",
            flops=2 * 1536 * 1024 * 256,
        )
        swapped = send(other, "core")
        if not last:
            half = mine + swapped
            parts = [half] + [send(half, "y", k) for k in (1, 2, 3)]
            half, gram = call(functools.partial(sum_kernel, 4), [shape(256, 128), shape(32, 128)], parts, name="sum")
            (inv,) = call(inverse_kernel, [shape(128, 128)], [gram], name="inverse", flops=10**9)
            right_args = [half, send(half, "core"), inv]
            lefts = [first_left] + list(more)
    messages = call(message_kernel, [shape(96, 128)] * 4, [place, mine, swapped], name="messages")
    parts = [messages[0]] + [send(messages[k], "y", k) for k in (1, 2, 3)]
    (time_out,) = call(final_kernel, [shape(64, 128)], parts, name="final")

    return outliers, first_left.T, time_out.T


def solution(mesh):
    in_specs = (P("chan", "tm"), P(("chan", "tm"), None), P(("tm", "chan"), None))
    out_specs = (P("chan", "tm"), P(("chan", "tm"), None), P(("tm", "chan"), None))
    return jax.shard_map(shards, mesh=mesh, in_specs=in_specs, out_specs=out_specs, check_vma=False)
```

```python
import functools

import jax
import jax.numpy as jnp
import numpy as np
from jax import lax
from jax.experimental import pallas as pl
from jax.experimental.pallas import tpu as pltpu
from jax.sharding import PartitionSpec as P

THRESHOLD = 1.5
RIDGE = 8.0
RANK = 64
PIECE = 128
F32 = jnp.float32
BF16 = jnp.bfloat16
AXES = ("chan", "tm")
MIB = 1 << 20


def exact(first, second, dims):
    return lax.dot_general(
        first,
        second,
        (dims, ((), ())),
        precision=lax.Precision.HIGHEST,
        preferred_element_type=F32,
    )


def single(first, second, dims):
    return lax.dot_general(first, second, (dims, ((), ())), preferred_element_type=F32)


def low_lanes(shape):
    return lax.broadcasted_iota(jnp.int32, shape, 1) < RANK


def two_parts(values):
    high = values.astype(BF16)
    return high, (values - high.astype(F32)).astype(BF16)


def row_stack(packed):
    low = low_lanes(packed.shape)
    high = packed.astype(BF16).astype(F32)
    rest = packed - high
    first = jnp.where(low, high, pltpu.roll(rest, RANK, 1))
    second = jnp.where(low, pltpu.roll(high, RANK, 1), rest)
    return jnp.concatenate([first, second], axis=0).astype(BF16)


def gram_of(stack):
    four = single(stack, stack, ((1,), (1,)))
    two = four[:RANK] + four[RANK:]
    return two[:, :RANK] + two[:, RANK:]


def pack_gram(gram):
    return jnp.concatenate([gram[:32], gram[32:]], axis=1)


def solve_rows(rows, e):
    n = len(rows)
    for t in range(0, n, 2):
        a, b, c, d = e[t][t], e[t][t + 1], e[t + 1][t], e[t + 1][t + 1]
        scale = 1.0 / (a * d - b * c)
        a, b, c, d = a * scale, b * scale, c * scale, d * scale
        rows[t], rows[t + 1] = d * rows[t] - b * rows[t + 1], a * rows[t + 1] - c * rows[t]
        for j in range(t + 2, n):
            e[t][j], e[t + 1][j] = d * e[t][j] - b * e[t + 1][j], a * e[t + 1][j] - c * e[t][j]
        for i in range(n):
            if i in (t, t + 1):
                continue
            f, g = e[i][t], e[i][t + 1]
            rows[i] = rows[i] - (f * rows[t] + g * rows[t + 1])
            for j in range(t + 2, n):
                e[i][j] = e[i][j] - (f * e[t][j] + g * e[t + 1][j])
    return rows


def inverse(packed):
    flat = jnp.concatenate([packed, pltpu.roll(packed, RANK, 1)], axis=0)
    row = lax.broadcasted_iota(jnp.int32, (RANK, 2 * RANK), 0)
    lane = lax.broadcasted_iota(jnp.int32, (RANK, 2 * RANK), 1)
    flat = jnp.where(lane < RANK, flat, 0.0)
    flat = flat + jnp.where(lane == row, RIDGE, 0.0)
    flat = flat + jnp.where(lane == row + RANK, 1.0, 0.0)
    full = (8, 2 * RANK)
    blocks = [flat[8 * b : 8 * b + 8] for b in range(8)]
    sub = lax.broadcasted_iota(jnp.int32, full, 0)
    for b in range(8):
        k = 8 * b
        rows = [jnp.broadcast_to(blocks[b][i : i + 1], full) for i in range(8)]
        entries = [[jnp.broadcast_to(r[:, k + j : k + j + 1], full) for j in range(8)] for r in rows]
        rows = solve_rows(rows, entries)
        for i in range(8):
            changed = blocks[i]
            for j in range(8):
                if i == b:
                    changed = jnp.where(sub == j, rows[j], changed)
                else:
                    changed = changed - jnp.broadcast_to(blocks[i][:, k + j : k + j + 1], full) * rows[j]
            blocks[i] = changed
    return jnp.concatenate(blocks, axis=0)


def quarter_kernel(place_ref, *refs):
    v = place_ref[3]
    for k in range(4):
        rows = pl.ds(pl.multiple_of(lax.rem(v + 4 - k, 4) * RANK, RANK), RANK)
        piece = refs[k][...].T
        refs[-1][rows] = jnp.concatenate([piece[:RANK], piece[RANK:]], axis=1)


def right_kernel(start, place_ref, *refs):
    if start:
        owns, others = refs[:4], refs[4:8]
        refs = refs[8:]
    else:
        mine_ref, other_ref, inv_ref = refs[:3]
        refs = refs[3:]
    wide_ref, tall_ref, gram_ref, held = refs
    y, core = place_ref[0], place_ref[1]
    for k in range(4):
        spot = lax.rem(y + 4 - k, 4) if start else k
        if start:
            own, other = owns[k][...], others[k][...]
        else:
            own, other = mine_ref[RANK * k : RANK * (k + 1)], other_ref[RANK * k : RANK * (k + 1)]
        held[2 * spot + core] = own
        held[2 * spot + 1 - core] = other
    full = jnp.concatenate([held[c] for c in range(8)], axis=1)
    if not start:
        full = exact(inv_ref[:RANK, :RANK], full, ((1,), (0,)))
    high, low = two_parts(full)
    gram_ref[...] = pack_gram(gram_of(jnp.concatenate([high, low], axis=0)))
    wide_ref[0:64] = high
    wide_ref[64:128] = high
    wide_ref[128:192] = low
    wide_ref[192:256] = low
    tall_ref[0:64] = high
    tall_ref[64:128] = low


def piece_of(core, q, i):
    return jnp.where(core == 0, 4 * q + i, 4 * i + q)


def rows_kernel(j, place_ref, a_ref, left_ref, wide_ref, tall_ref, gram_ref, s_ref, h_ref, l_ref):
    core, u = place_ref[1], place_ref[2]
    q = lax.rem(u + j + 1, 4)
    low = low_lanes((RANK, PIECE))
    for half in range(2):
        spots = []
        stacks = []
        for i in (2 * half, 2 * half + 1):
            p = piece_of(core, q, i)
            spots.append(pl.multiple_of(p * PIECE, PIECE))
            packed = left_ref[RANK * i : RANK * (i + 1)]
            stacks.append(row_stack(packed))
        stack = jnp.concatenate(stacks, axis=0)
        stack = jnp.concatenate([stack, stack], axis=1)
        product = single(stack, wide_ref[...], ((1,), (0,)))
        values = jnp.concatenate([a_ref[pl.ds(s, PIECE)] for s in spots], axis=0)
        cleaned = product + jnp.clip(values - product, -THRESHOLD, THRESHOLD)
        high, rest = two_parts(cleaned)
        for n in range(2):
            i = 2 * half + n
            for part, ref in ((high, h_ref), (rest, l_ref)):
                ref[64 * i : 64 * i + 64] = part[128 * n : 128 * n + 64]
                ref[256 + 64 * i : 320 + 64 * i] = part[128 * n + 64 : 128 * n + 128]
        total = single(high, tall_ref[...], ((1,), (1,))) + single(rest, tall_ref[...], ((1,), (1,)))
        total = total + pltpu.roll(total, RANK, 1)
        for n in range(2):
            i = 2 * half + n
            s_ref[64 * i : 64 * i + 64] = jnp.where(low, total[128 * n : 128 * n + 64], total[128 * n + 64 : 128 * n + 128])
    s_ref[256:288] = gram_ref[...]


def inverse_kernel(sum_ref, inv_ref):
    found = inverse(sum_ref[...])
    low = low_lanes((RANK, PIECE))
    inv_ref[0:64] = jnp.where(low, pltpu.roll(found, RANK, 1), 0.0)
    inv_ref[64:128] = jnp.where(low, 0.0, found)


def cols_kernel(count, has_acc, last, place_ref, inv_ref, *refs):
    s_refs, h_refs, l_refs = refs[:count], refs[count : 2 * count], refs[2 * count : 3 * count]
    refs = refs[3 * count :]
    if has_acc:
        acc_ref, acc_gram_ref = refs[:2]
        refs = refs[2:]
        mine_ref, other_ref = refs[:2]
    else:
        t_ref, gram_ref = refs[:2]
    left_refs = refs[2:]
    core, v = place_ref[1], place_ref[3]
    inv = inv_ref[...]
    gram = acc_gram_ref[...] if has_acc else jnp.zeros((RANK, RANK), F32)
    stacks = []
    for k in range(count):
        packed = exact(s_refs[k][0:256], inv, ((1,), (0,)))
        if not last:
            left_refs[k][...] = packed
        elif not has_acc:
            held = left_refs[1]
            held[...] = packed
            own = held[pl.ds(pl.multiple_of(v * RANK, RANK), RANK)]
            left_refs[0][...] = jnp.concatenate([own[:, :RANK], own[:, RANK:]], axis=0).T
        turned = packed.T
        turned = jnp.concatenate([turned[:RANK], turned[RANK:]], axis=1)
        stack = jnp.concatenate(two_parts(turned), axis=0)
        gram += gram_of(stack) if count == 1 else exact(turned, turned, ((1,), (1,)))
        stacks.append(stack)
    tiles = []
    for t in range(4):
        cols = slice(256 * t, 256 * t + 256)
        total = jnp.zeros((PIECE, 256), F32)
        for k in range(count):
            total += single(stacks[k], h_refs[k][:, cols], ((1,), (0,)))
            total += single(stacks[k], l_refs[k][:, cols], ((1,), (0,)))
        part = total[:RANK] + total[RANK:]
        if has_acc:
            part += acc_ref[:, cols]
            even, odd = part[:, :PIECE], part[:, PIECE:]
            mine_ref[RANK * t : RANK * (t + 1)] = jnp.where(core == 0, even, odd)
            other_ref[RANK * t : RANK * (t + 1)] = jnp.where(core == 0, odd, even)
        else:
            t_ref[:, cols] = part
    if has_acc:
        mine_ref[256:288] = pack_gram(gram)
        other_ref[256:288] = pack_gram(gram)
    else:
        gram_ref[...] = gram


def message_kernel(place_ref, first_ref, second_ref, *out_refs):
    y = place_ref[0]
    gram = first_ref[256:288] + second_ref[256:288]
    for k in range(4):
        rows = pl.ds(pl.multiple_of(lax.rem(y + k, 4) * RANK, RANK), RANK)
        out_refs[k][0:64] = first_ref[rows] + second_ref[rows]
        out_refs[k][64:96] = gram


def final_kernel(m0, m1, m2, m3, out_ref):
    total = m0[...] + m1[...] + m2[...] + m3[...]
    found = inverse(total[64:96])[:, RANK:]
    out_ref[...] = exact(found, total[:64], ((1,), (0,)))


def outlier_kernel(spots_ref, left_ref, wide_ref, a_ref, after_ref, out_ref, token_ref):
    g = pl.program_id(0)
    stacks = []
    for n in range(2):
        spot = pl.multiple_of(spots_ref[4 + 2 * g + n] * RANK, RANK)
        stacks.append(row_stack(left_ref[pl.ds(spot, RANK)]))
    stack = jnp.concatenate(stacks, axis=0)
    stack = jnp.concatenate([stack, stack], axis=1)
    rows = pl.ds(pl.multiple_of(g * 256, 256), 256)
    for t in range(2):
        cols = slice(512 * t, 512 * t + 512)
        residue = a_ref[rows, cols] - single(stack, wide_ref[:, cols], ((1,), (0,)))
        out_ref[:, cols] = residue - jnp.clip(residue, -THRESHOLD, THRESHOLD)
    token_ref[...] = jnp.zeros_like(token_ref)


def sum_kernel(count, *refs):
    total = refs[0][...]
    for ref in refs[1:count]:
        total = total + ref[...]
    refs[-2][...] = total[:256]
    refs[-1][...] = total[256:]


VM = pl.BlockSpec(memory_space=pltpu.VMEM)
SM = pl.BlockSpec(memory_space=pltpu.SMEM)
ANY = pl.BlockSpec(memory_space=pl.ANY)


def shape(*dims, dtype=F32):
    return jax.ShapeDtypeStruct(dims, dtype)


def call(kernel, outs, args, scratch=(), name=None, flops=0, limit=16):
    return pl.pallas_call(
        kernel,
        out_shape=outs,
        in_specs=[SM if a.dtype == jnp.int32 else VM for a in args],
        out_specs=[VM for _ in outs],
        scratch_shapes=list(scratch),
        compiler_params=pltpu.CompilerParams(vmem_limit_bytes=limit * MIB),
        cost_estimate=pl.CostEstimate(flops=flops, bytes_accessed=MIB, transcendentals=0),
        name=name,
    )(*args)


def ring(kind, k):
    pairs = []
    for chan in range(8):
        for tm in range(16):
            y, core = divmod(chan, 2)
            x, z = divmod(tm, 4)
            axis = kind
            if kind == "u":
                axis = "xz"[core]
            elif kind == "v":
                axis = "zx"[core]
            if axis == "x":
                x = (x + k) % 4
            elif axis == "z":
                z = (z + k) % 4
            elif axis == "y":
                y = (y + k) % 4
            else:
                core = 1 - core
            pairs.append((chan * 16 + tm, (2 * y + core) * 16 + 4 * x + z))
    return pairs


def send(values, kind, k=1):
    return lax.ppermute(values, AXES, ring(kind, k))


def places():
    table = np.zeros((128, 20), np.int32)
    for chan in range(8):
        for tm in range(16):
            y, core = divmod(chan, 2)
            x, z = divmod(tm, 4)
            u, v = (x, z) if core == 0 else (z, x)
            spots = []
            for p in range(16):
                q, i = divmod(p, 4)
                if core == 1:
                    q, i = i, q
                spots.append((u - q) % 4 * 4 + i)
            table[chan * 16 + tm] = [y, core, u, v] + spots
    return table


def shards(readings, channel_start, time_start):
    chan, tm = lax.axis_index("chan"), lax.axis_index("tm")
    place = lax.dynamic_index_in_dim(jnp.asarray(places()), chan * 16 + tm, keepdims=False)

    chan_piece, time_piece = channel_start.T, time_start.T
    lefts = [chan_piece] + [send(chan_piece, "v", k) for k in (1, 2, 3)]
    owns = [time_piece] + [send(time_piece, "y", k) for k in (1, 2, 3)]
    (left_own,) = call(quarter_kernel, [shape(256, 128)], [place] + lefts + owns[1:], name="quarter", flops=5 * 10**9)
    lefts = [left_own] + [send(left_own, "u", k) for k in (1, 2, 3)]
    others = [send(piece, "core") for piece in owns]
    right_args = owns + others
    for sweep in range(2):
        start, last = sweep == 0, sweep == 1
        wide, tall, gram = call(
            functools.partial(right_kernel, start),
            [shape(256, 1024, dtype=BF16), shape(128, 1024, dtype=BF16), shape(32, 128)],
            [place] + list(right_args),
            scratch=[pltpu.VMEM((8, 64, 128), F32)],
            name="right",
            flops=5 * 10**9,
        )
        sums, highs, rests = [], [], []
        for j in range(4):
            s, h, r = call(
                functools.partial(rows_kernel, j),
                [shape(288, 128), pltpu.VMEM((512, 1024), BF16), pltpu.VMEM((512, 1024), BF16)],
                [place, readings, lefts[3 - j], wide, tall, gram],
                name="rows",
                flops=2 * 512 * 1024 * 768,
            )
            sums.append(s)
            highs.append(h)
            rests.append(r)
        got = [send(sums[k - 1], "u", k) for k in (1, 2, 3)]
        own = sums[3] + got[0] + got[1] + got[2]
        if last:
            outliers, token = pl.pallas_call(
                outlier_kernel,
                out_shape=[shape(2048, 1024), shape(8, 128)],
                grid_spec=pltpu.PrefetchScalarGridSpec(
                    num_scalar_prefetch=1,
                    grid=(8,),
                    in_specs=[
                        pl.BlockSpec((1024, 128), lambda g, spots: (0, 0)),
                        pl.BlockSpec((256, 1024), lambda g, spots: (0, 0)),
                        VM,
                        ANY,
                    ],
                    out_specs=[
                        pl.BlockSpec((256, 1024), lambda g, spots: (g, 0)),
                        pl.BlockSpec((8, 128), lambda g, spots: (0, 0)),
                    ],
                ),
                compiler_params=pltpu.CompilerParams(vmem_limit_bytes=12 * MIB),
                cost_estimate=pl.CostEstimate(flops=2 * 2048 * 1024 * 256, bytes_accessed=16 * MIB, transcendentals=0),
                name="outliers",
            )(place, jnp.concatenate(lefts, axis=0), wide, readings, own)
        parts = [own] + [send(own, "v", k) for k in (1, 2, 3)]
        own, gram = call(functools.partial(sum_kernel, 4), [shape(256, 128), shape(32, 128)], parts + ([token] if last else []), name="sum")
        (inv,) = call(inverse_kernel, [shape(128, 128)], [gram], name="inverse", flops=10**9)
        quarters = [own] + [send(own, "u", k) for k in (1, 2, 3)]
        first_outs = [shape(64, 1024), shape(64, 64)]
        first_scratch = []
        if last:
            first_outs.append(shape(64, 128))
            first_scratch.append(pltpu.VMEM((256, 128), F32))
        else:
            first_outs.append(shape(256, 128))
        acc, acc_gram, first_left = call(
            functools.partial(cols_kernel, 1, False, last),
            first_outs,
            [place, inv, own, highs[3], rests[3]],
            scratch=first_scratch,
            name="cols_own",
            flops=2 * 512 * 1024 * 256,
        )
        order = (2, 1, 0)
        outs = [shape(288, 128), shape(288, 128)] + ([] if last else [shape(256, 128)] * 3)
        mine, other, *more = call(
            functools.partial(cols_kernel, 3, True, last),
            outs,
            [place, inv] + quarters[1:] + [highs[i] for i in order] + [rests[i] for i in order] + [acc, acc_gram],
            name="cols_rest",
            flops=2 * 1536 * 1024 * 256,
        )
        swapped = send(other, "core")
        if not last:
            half = mine + swapped
            parts = [half] + [send(half, "y", k) for k in (1, 2, 3)]
            half, gram = call(functools.partial(sum_kernel, 4), [shape(256, 128), shape(32, 128)], parts, name="sum")
            (inv,) = call(inverse_kernel, [shape(128, 128)], [gram], name="inverse", flops=10**9)
            right_args = [half, send(half, "core"), inv]
            lefts = [first_left] + list(more)
    messages = call(message_kernel, [shape(96, 128)] * 4, [place, mine, swapped], name="messages")
    parts = [messages[0]] + [send(messages[k], "y", k) for k in (1, 2, 3)]
    (time_out,) = call(final_kernel, [shape(64, 128)], parts, name="final")

    return outliers, first_left.T, time_out.T


def solution(mesh):
    in_specs = (P("chan", "tm"), P(("chan", "tm"), None), P(("tm", "chan"), None))
    out_specs = (P("chan", "tm"), P(("chan", "tm"), None), P(("tm", "chan"), None))
    return jax.shard_map(shards, mesh=mesh, in_specs=in_specs, out_specs=out_specs, check_vma=False)
```
